256 devices in a mesh: cp: 64 (over y, z, core), hd: 4 (over x).
Axes of the slice: x: 4, y: 4, z: 8, core: 2. Of those that a mesh axis runs over, the one named last changes fastest.
Arguments:
- query_projection: bfloat16 [32768, 8192], P(('cp', 'hd')), may hold values from -8 to 8
- key_projection: bfloat16 [32768, 1024], P(('cp', 'hd')), may hold values from -8 to 8
- value_projection: bfloat16 [32768, 1024], P(('cp', 'hd')), may hold values from -6 to 6
- output_gradient: bfloat16 [32768, 8192], P(('cp', 'hd')), may hold values from -6 to 6
- doc_ids: int32 [32768], replicated, may hold values from 0 to 127, never falling along the last dimension, each value on 1 to 512 neighbouring positions
- tile_plan: int32 [64], replicated, may hold values from 0 to 2, as said below
Outputs:
- query_grad: bfloat16 [32768, 8192], P('cp', 'hd')
- key_gradient: bfloat16 [32768, 1024], P('cp', 'hd')
- value_gradient: bfloat16 [32768, 1024], P('cp', 'hd')
The draws below stay inside these ranges and needn't reach their ends.
Inputs may be any that keep to these rules, and one draw needn't show every extreme that they name: `doc_ids`: document ids never fall; every document has at most 512 tokens, and one has exactly 512. `tile_plan`: entry 0 and entry 62 are 0; entry 1 and the last entry are 2; where an entry is 2, the entry before it is 0.
All inputs are finite; a program needn't handle non-finite values.
Results may differ from the reference program's by a relative error of at most 0.007.
Values may be sent and summed in bfloat16 or wider, within the bound.
No kernel may reach another device: no remote copies, remote signals or barrier semaphores. Data moves between devices by JAX's collectives and lax.ppermute only.
A program may use at most 256 MiB of HBM per device.

```python
import math
import jax
import jax.numpy as jnp
import numpy as np
from jax import lax

QUERY_HEADS = 64
KEY_VALUE_HEADS = 8
HEAD_DIM = 128
BLOCK_TOKENS = 512
BLOCKS = 64
SEQUENCE_LENGTH = 32768
MOST = 512
N_CP = 64


def draw_query_projection(key, part):
    key = jax.random.fold_in(key, 1)
    heads_per_group = QUERY_HEADS // KEY_VALUE_HEADS
    base_offset = jnp.clip(jax.random.normal(key, (SEQUENCE_LENGTH, KEY_VALUE_HEADS, heads_per_group, HEAD_DIM), jnp.float32), -6.0, 6.0)
    return base_offset.reshape(SEQUENCE_LENGTH, QUERY_HEADS * HEAD_DIM).astype(jnp.bfloat16)


def draw_key_projection(key, part):
    key = jax.random.fold_in(key, 2)
    base_offset = jnp.clip(jax.random.normal(key, (SEQUENCE_LENGTH, KEY_VALUE_HEADS, HEAD_DIM), jnp.float32), -6.0, 6.0)
    return base_offset.reshape(SEQUENCE_LENGTH, KEY_VALUE_HEADS * HEAD_DIM).astype(jnp.bfloat16)


def draw_tile_plan(key, part):
    key = jax.random.fold_in(key, 7)
    places = jnp.arange(BLOCKS, dtype=jnp.int32)
    raw = jax.random.randint(key, (BLOCKS,), 0, 3, jnp.int32)
    raw = jnp.where(places == 0, 0, raw)
    raw = jnp.where(places == 1, 2, raw)
    raw = jnp.where(places == BLOCKS - 2, 0, raw)
    raw = jnp.where(places == BLOCKS - 1, 2, raw)
    before = jnp.concatenate([jnp.zeros((1,), jnp.int32), raw[:-1]], axis=0)
    return jnp.where((raw == 2) & (before != 0), 1, raw).astype(jnp.int32)


def level_of(stream_key, dims, pieces, smallest, largest):
    gain, own = 1.0, jax.random.fold_in(stream_key, 6)
    for axis_at, shards_of in pieces:
        draws = jnp.exp(jax.random.uniform(jax.random.fold_in(own, axis_at), (shards_of,), jnp.float32, smallest / len(pieces), largest / len(pieces)))
        gain = gain * jnp.repeat(draws, dims[axis_at] // shards_of).reshape([-1 if axis == axis_at else 1 for axis in range(len(dims))])
    return gain


def profile(count, total, reach, lean):
    weights = [(1 << 20) // math.isqrt(standing ** lean) + 1 for standing in range(2, count + 1)]
    rest, given = total - reach - (count - 1), [1] * (count - 1)
    while rest > 0:
        free = [i for i in range(count - 1) if given[i] < reach]
        mass, budget = sum([weights[i] for i in free]), rest
        for i in free:
            addition = min(reach - given[i], max(1, budget * weights[i] // mass), rest)
            given[i] = given[i] + addition
            rest = rest - addition
    return np.array([reach] + given)


def uneven_parts(own_key, number_of, total, most, slope):
    if number_of == 2:
        one = jax.random.randint(own_key, (), max(1, total - most), min(most, total - 1) + 1)
        return jnp.stack([one, total - one])
    sizes = jnp.asarray(profile(number_of, total, most, slope), jnp.int32)
    pairs = (number_of - 1) // 2
    donor, receiver = sizes[1:1 + 2 * pairs:2], sizes[2:2 + 2 * pairs:2]
    room = jnp.minimum(donor - 1, most - receiver)
    passed = jax.random.randint(jax.random.fold_in(own_key, 1), (pairs,), 0, 1 << 20) % (room + 1)
    sizes = sizes.at[1:1 + 2 * pairs:2].set(donor - passed).at[2:2 + 2 * pairs:2].set(receiver + passed)
    return sizes[jax.random.permutation(jax.random.fold_in(own_key, 2), number_of)]


def bell_draw(stream_key, shape, scale, bound, cuts=(), held_as=jnp.bfloat16):
    level = level_of(stream_key, shape, cuts, -0.22, 0.18) if cuts else 1.0
    values = jax.random.normal(stream_key, shape, jnp.float32) * scale * level
    return jnp.minimum(jnp.maximum(values, -bound), bound).astype(held_as)


def setup_inputs(seed: int = 0) -> dict:
    splits = jax.random.split(jax.random.key(seed), 7)
    query_projection = draw_query_projection(jax.random.fold_in(splits[6], 71), 0)
    key_projection = draw_key_projection(jax.random.fold_in(splits[6], 71), 0)
    value_projection = bell_draw(splits[2], (SEQUENCE_LENGTH, KEY_VALUE_HEADS * HEAD_DIM), 1.0, 6.0, ((0, 256),))
    output_gradient = bell_draw(splits[3], (SEQUENCE_LENGTH, QUERY_HEADS * HEAD_DIM), 1.0, 6.0, ((0, 256),))
    doc_ids = jnp.searchsorted(jnp.cumsum(uneven_parts(splits[4], 2 * BLOCKS, SEQUENCE_LENGTH, MOST, 1)), jnp.arange(SEQUENCE_LENGTH), side="right").astype(jnp.int32)
    tile_plan = draw_tile_plan(jax.random.fold_in(splits[6], 71), 0)
    return {"query_projection": query_projection, "key_projection": key_projection, "value_projection": value_projection, "output_gradient": output_gradient, "doc_ids": doc_ids, "tile_plan": tile_plan}


def block_grads(query_blk, dout_blk, key_window, value_window, allowed):
    inv_root = 1.0 / math.sqrt(HEAD_DIM)
    query_f = query_blk.astype(jnp.float32)
    dout_f = dout_blk.astype(jnp.float32)
    key_f = key_window.astype(jnp.float32)
    value_f = value_window.astype(jnp.float32)
    scores = jnp.einsum('tkgd,skd->kgts', query_f, key_f) * inv_root
    masked = jnp.where(allowed, scores, -1e+30)
    highest = lax.optimization_barrier(jnp.max(masked, axis=-1, keepdims=True))
    total = lax.optimization_barrier(jnp.sum(jnp.where(allowed, jnp.exp(masked - highest), 0.0), axis=-1, keepdims=True))
    log_norm = highest + jnp.log(total)
    probs = jnp.where(allowed, jnp.exp(scores - log_norm), 0.0)
    dprobs = jnp.einsum('tkgd,skd->kgts', dout_f, value_f)
    delta = lax.optimization_barrier(jnp.sum(probs * dprobs, axis=-1, keepdims=True))
    dscores = (probs * (dprobs - delta) * inv_root).astype(jnp.bfloat16).astype(jnp.float32)
    probs_low = probs.astype(jnp.bfloat16).astype(jnp.float32)
    query_gradient_out = jnp.einsum('kgts,skd->tkgd', dscores, key_f)
    key_gradient_out = jnp.einsum('kgts,tkgd->skd', dscores, query_f)
    value_gradient_out = jnp.einsum('kgts,tkgd->skd', probs_low, dout_f)
    return (query_gradient_out, key_gradient_out, value_gradient_out)

def reference(query_projection, key_projection, value_projection, output_gradient, doc_ids, tile_plan):
    heads_per_group = QUERY_HEADS // KEY_VALUE_HEADS
    window_width = 2 * BLOCK_TOKENS
    key_padded = jnp.concatenate([jnp.zeros((BLOCK_TOKENS, KEY_VALUE_HEADS * HEAD_DIM), key_projection.dtype), key_projection], axis=0)
    value_padded = jnp.concatenate([jnp.zeros((BLOCK_TOKENS, KEY_VALUE_HEADS * HEAD_DIM), value_projection.dtype), value_projection], axis=0)
    doc_all = doc_ids.astype(jnp.int32)
    doc_pad = jnp.concatenate([jnp.full((BLOCK_TOKENS,), -1, jnp.int32), doc_all], axis=0)
    query_row_blocks = query_projection.reshape(N_CP, BLOCK_TOKENS, KEY_VALUE_HEADS, heads_per_group, HEAD_DIM)
    output_grad_blocks = output_gradient.reshape(N_CP, BLOCK_TOKENS, KEY_VALUE_HEADS, heads_per_group, HEAD_DIM)
    local_rows = jnp.arange(BLOCK_TOKENS, dtype=jnp.int32)
    local_keys = jnp.arange(window_width, dtype=jnp.int32) - BLOCK_TOKENS
    earlier_part = jnp.arange(window_width, dtype=jnp.int32) < BLOCK_TOKENS

    def one_block(items):
        index, query_blk, dout_blk, plan_entry = items
        start_offset = (index * BLOCK_TOKENS).astype(jnp.int32)
        key_window = lax.dynamic_slice_in_dim(key_padded, start_offset, window_width, 0).reshape(window_width, KEY_VALUE_HEADS, HEAD_DIM)
        value_window = lax.dynamic_slice_in_dim(value_padded, start_offset, window_width, 0).reshape(window_width, KEY_VALUE_HEADS, HEAD_DIM)
        key_docs = lax.dynamic_slice_in_dim(doc_pad, start_offset, window_width, 0)
        query_docs = lax.dynamic_slice_in_dim(doc_all, start_offset, BLOCK_TOKENS, 0)
        tile_ok = jnp.where(earlier_part, plan_entry != 0, True)
        allowed = (query_docs[:, None] == key_docs[None, :]) & (local_keys[None, :] <= local_rows[:, None]) & tile_ok[None, :]
        query_gradient_out, key_gradient_out, value_gradient_out = block_grads(query_blk, dout_blk, key_window, value_window, allowed)
        return (query_gradient_out.reshape(BLOCK_TOKENS, QUERY_HEADS * HEAD_DIM).astype(jnp.bfloat16), key_gradient_out.reshape(window_width, KEY_VALUE_HEADS * HEAD_DIM), value_gradient_out.reshape(window_width, KEY_VALUE_HEADS * HEAD_DIM))
    indices = jnp.arange(N_CP, dtype=jnp.int32)
    query_all, key_gathered, value_gathered = lax.map(one_block, (indices, query_row_blocks, output_grad_blocks, tile_plan.astype(jnp.int32)))
    key_gathered = key_gathered.reshape(N_CP, 2, BLOCK_TOKENS, KEY_VALUE_HEADS * HEAD_DIM)
    value_gathered = value_gathered.reshape(N_CP, 2, BLOCK_TOKENS, KEY_VALUE_HEADS * HEAD_DIM)
    padding_filler = jnp.zeros((1, BLOCK_TOKENS, KEY_VALUE_HEADS * HEAD_DIM), jnp.float32)
    key_grand_total = key_gathered[:, 1] + jnp.concatenate([key_gathered[1:, 0], padding_filler], axis=0)
    value_grand_total = value_gathered[:, 1] + jnp.concatenate([value_gathered[1:, 0], padding_filler], axis=0)
    query_grad = query_all.reshape(SEQUENCE_LENGTH, QUERY_HEADS * HEAD_DIM)
    key_gradient = key_grand_total.reshape(SEQUENCE_LENGTH, KEY_VALUE_HEADS * HEAD_DIM).astype(jnp.bfloat16)
    value_gradient = value_grand_total.reshape(SEQUENCE_LENGTH, KEY_VALUE_HEADS * HEAD_DIM).astype(jnp.bfloat16)
    return (query_grad, key_gradient, value_gradient)
```

```python
import functools
import math

import jax
import jax.numpy as jnp
from jax import lax
from jax.experimental import pallas as pl
from jax.experimental.pallas import tpu as pltpu
from jax.sharding import PartitionSpec as P

HEAD_DIM = 128
TILE = 128
STACK = 4
SHIFTS = (1, -1, 2)
PARTS = ((0, 0, 8), (1, 0, 4), (1, 4, 4))

ANY = pl.BlockSpec(memory_space=pl.ANY)
VMEM = pl.BlockSpec(memory_space=pltpu.VMEM)
SMEM = pl.BlockSpec(memory_space=pltpu.SMEM)
ROWS_BY_ROWS = (((1,), (1,)), ((), ()))
ROWS_BY_COLUMNS = (((1,), (0,)), ((), ()))


def dot(left, right, dims):
    return lax.dot_general(left, right, dims, preferred_element_type=jnp.float32)


def aligned(index, unit):
    return pl.multiple_of(index * unit, unit)


def source_of(me, shift):
    return lax.rem(me - shift + 4, 4)


def run_copies(pairs, staging, sems):
    ins = [
        pltpu.make_async_copy(src, staging.at[i], sems.at[0, i]) for i, (src, _) in enumerate(pairs)
    ]
    outs = [
        pltpu.make_async_copy(staging.at[i], dst, sems.at[1, i]) for i, (_, dst) in enumerate(pairs)
    ]
    for copy in ins:
        copy.start()
    for i, copy in enumerate(ins):
        copy.wait()
        outs[i].start()
    for copy in outs:
        copy.wait()


def cut_pairs(me, pieces, outs):
    pairs = []
    for shift, out in zip(SHIFTS, outs):
        to = lax.rem(me + shift + 4, 4)
        for at, (array, share, first, width) in enumerate(pieces):
            column = pl.multiple_of(to * share + first, TILE)
            pairs.append((array.at[:, pl.ds(column, width)], out.at[at]))
    return pairs


def cut_kernel(shares, me_ref, left, right, out_a, out_b, out_c, staging, sems):
    pieces = [(array, *shares) for array in (left, right)]
    run_copies(cut_pairs(me_ref[0], pieces, (out_a, out_b, out_c)), staging, sems)


def cut(me, left, right, share, first, width):
    rows = left.shape[0]
    shape = jax.ShapeDtypeStruct((2, rows, width), left.dtype)
    return pl.pallas_call(
        functools.partial(cut_kernel, (share, first, width)),
        out_shape=(shape,) * 3,
        in_specs=[SMEM, ANY, ANY],
        out_specs=(ANY,) * 3,
        scratch_shapes=[
            pltpu.VMEM((6, rows, width), left.dtype),
            pltpu.SemaphoreType.DMA((2, 6)),
        ],
        cost_estimate=pl.CostEstimate(
            flops=0, bytes_accessed=12 * rows * width * 2, transcendentals=0
        ),
    )(me, left, right)


def join_kernel(width, me_ref, got_a, got_b, got_c, left, right, out, staging, sems):
    me = me_ref[0]
    rows = left.shape[0]
    pairs = []
    for shift, got in zip(SHIFTS, (got_a, got_b, got_c)):
        at = pl.ds(aligned(source_of(me, shift), rows), rows)
        pairs += [(got.at[i], out.at[i, at, :]) for i in range(2)]
    at = pl.ds(aligned(me, rows), rows)
    columns = pl.ds(aligned(me, width), width)
    pairs += [(array.at[:, columns], out.at[i, at, :]) for i, array in enumerate((left, right))]
    run_copies(pairs, staging, sems)


def join(me, got, left, right):
    rows, width = got[0].shape[1:]
    return pl.pallas_call(
        functools.partial(join_kernel, width),
        out_shape=jax.ShapeDtypeStruct((2, 4 * rows, width), left.dtype),
        in_specs=[SMEM] + [ANY] * 5,
        out_specs=ANY,
        scratch_shapes=[
            pltpu.VMEM((8, rows, width), left.dtype),
            pltpu.SemaphoreType.DMA((2, 8)),
        ],
        cost_estimate=pl.CostEstimate(
            flops=0, bytes_accessed=16 * rows * width * 2, transcendentals=0
        ),
    )(me, *got, left, right)


def attention_kernel(part, has_query, has_sums, ends, *refs):
    group, first, heads = part
    stacks = heads // STACK
    wide = STACK * HEAD_DIM
    refs = list(refs)
    scal, start, kv_own, kv_prev, got_a, got_b, got_c, query, dout = refs[:9]
    refs = refs[9 + has_query :]
    if has_sums:
        sums_in = refs.pop(0)
    query_out = refs.pop(0)
    if ends:
        own_out, prior_out = refs.pop(0), refs.pop(0)
    else:
        sums_out = refs.pop(0)
    q_all, d_all, keys, values, keys_t, bias, sums, dq, kv_sems, in_sems, out_sems = refs
    me = scal[0]
    rows = query.shape[0]
    block = 4 * rows

    kv_copies = []
    for i, target in enumerate((keys, values)):
        for j, source in enumerate((kv_prev, kv_own)):
            kv_copies.append(
                pltpu.make_async_copy(
                    source.at[i, :, pl.ds(group * HEAD_DIM, HEAD_DIM)],
                    target.at[pl.ds(j * block, block), :],
                    kv_sems.at[2 * i + j],
                )
            )
    if has_sums:
        kv_copies.append(pltpu.make_async_copy(sums_in, sums, kv_sems.at[4]))
    for copy in kv_copies:
        copy.start()
    in_copies = []
    for stack in range(stacks):
        some = []
        for i, (own, target) in enumerate(((query, q_all), (dout, d_all))):
            column = me * (2048) + (group * 8 + first + stack * STACK) * HEAD_DIM
            some.append((own.at[:, pl.ds(pl.multiple_of(column, TILE), wide)], target, i, me))
            for shift, got in zip(SHIFTS, (got_a, got_b, got_c)):
                piece = got.at[i, :, pl.ds(stack * wide, wide)]
                some.append((piece, target, i, source_of(me, shift)))
        copies = [
            pltpu.make_async_copy(
                source,
                target.at[stack, pl.ds(aligned(place, rows), rows), :],
                in_sems.at[8 * stack + at],
            )
            for at, (source, target, i, place) in enumerate(some)
        ]
        for copy in copies:
            copy.start()
        in_copies.append(copies)

    for row in range(4):
        place = lax.broadcasted_iota(jnp.int32, (5 * TILE, TILE), 0) + row * TILE
        token = lax.broadcasted_iota(jnp.int32, (5 * TILE, TILE), 1) + block + row * TILE
        since = start[:, row * TILE : (row + 1) * TILE]
        bias[row] = jnp.where((place >= since) & (place <= token), 0.0, -1e30)
    if not has_sums:
        sums[...] = jnp.zeros_like(sums)
    for copy in kv_copies:
        copy.wait()
    for i in range(8):
        piece = keys[i * TILE : (i + 1) * TILE, :]
        keys_t[i] = piece.astype(jnp.float32).T.astype(jnp.bfloat16)

    to_exponent = math.log2(math.e) / math.sqrt(HEAD_DIM)
    scale = 1.0 / math.sqrt(HEAD_DIM)

    def step(stack, row, tiles):
        size = tiles * TILE
        tile = row + 5 - tiles
        window = pl.ds(aligned(tile, TILE), size)
        own = pl.ds(aligned(row, TILE), TILE)
        key, value = keys[window, :], values[window, :]
        q = jnp.concatenate(
            [q_all[stack, own, h * HEAD_DIM : (h + 1) * HEAD_DIM] for h in range(STACK)], axis=0
        )
        d = jnp.concatenate(
            [d_all[stack, own, h * HEAD_DIM : (h + 1) * HEAD_DIM] for h in range(STACK)], axis=0
        )
        mask = bias[row, (5 - tiles) * TILE :, :]
        scores = dot(key, q, ROWS_BY_ROWS) * to_exponent + jnp.concatenate([mask] * STACK, axis=1)
        highest = jnp.max(scores, axis=0, keepdims=True)
        weights = jnp.exp2(scores - highest)
        probs = weights * (1.0 / jnp.sum(weights, axis=0, keepdims=True))
        dprobs = dot(value, d, ROWS_BY_ROWS)
        delta = jnp.sum(probs * dprobs, axis=0, keepdims=True)
        dscores = (probs * (dprobs - delta)).astype(jnp.bfloat16)
        sums[1, window, :] += dot(probs.astype(jnp.bfloat16), d, ROWS_BY_COLUMNS)
        sums[0, window, :] += dot(dscores, q, ROWS_BY_COLUMNS)
        key_t = jnp.concatenate([keys_t[tile + i] for i in range(tiles)], axis=1)
        dq_t = dot(key_t, dscores, ROWS_BY_COLUMNS) * scale
        for h in range(STACK):
            columns = slice(h * HEAD_DIM, (h + 1) * HEAD_DIM)
            dq[stack, own, columns] = dq_t[:, columns].T.astype(jnp.bfloat16)

    def out_copy(stack, row):
        own = pl.ds(aligned(row, TILE), TILE)
        column = (group * 8 + first + stack * STACK) * HEAD_DIM
        return pltpu.make_async_copy(
            dq.at[stack, own, :],
            query_out.at[own, pl.ds(column, wide)],
            out_sems.at[stack, row],
        )

    for stack in range(stacks):
        for copy in in_copies[stack]:
            copy.wait()

        @pl.loop(0, 4)
        def _(row):
            count = scal[1 + row]
            for tiles in range(1, 6):

                @pl.when(count == tiles)
                def _():
                    step(stack, row, tiles)

            out_copy(stack, row).start()

    if ends:
        own_out[0] = sums[0, block:, :] * scale
        own_out[1] = sums[1, block:, :]
        prior_out[0] = (sums[0, :block, :] * scale).astype(jnp.bfloat16)
        prior_out[1] = sums[1, :block, :].astype(jnp.bfloat16)
    else:
        sums_out[...] = sums[...]
    for stack in range(stacks):
        for row in range(4):
            out_copy(stack, row).wait()


def attention(part, scal, start, kv_own, kv_prev, got, query, dout, query_grad, sums, ends):
    group, first, heads = part
    rows = query.shape[0]
    block = 4 * rows
    stacks = heads // STACK
    wide = STACK * HEAD_DIM
    has_query, has_sums = query_grad is not None, sums is not None
    args = [scal, start, kv_own, kv_prev, *got, query, dout]
    specs = [SMEM, VMEM] + [ANY] * 7
    aliases = {}
    if has_query:
        aliases = {len(args): 0}
        args.append(query_grad)
        specs.append(ANY)
    if has_sums:
        args.append(sums)
        specs.append(ANY)
    shapes = [jax.ShapeDtypeStruct((block, 2048), jnp.bfloat16)]
    if ends:
        shapes.append(jax.ShapeDtypeStruct((2, block, HEAD_DIM), jnp.float32))
        shapes.append(jax.ShapeDtypeStruct((2, block, HEAD_DIM), jnp.bfloat16))
    else:
        shapes.append(jax.ShapeDtypeStruct((2, 2 * block, HEAD_DIM), jnp.float32))
    return pl.pallas_call(
        functools.partial(attention_kernel, part, has_query, has_sums, ends),
        out_shape=tuple(shapes),
        in_specs=specs,
        out_specs=(ANY,) + (VMEM,) * (len(shapes) - 1),
        scratch_shapes=[
            pltpu.VMEM((stacks, block, wide), jnp.bfloat16),
            pltpu.VMEM((stacks, block, wide), jnp.bfloat16),
            pltpu.VMEM((2 * block, HEAD_DIM), jnp.bfloat16),
            pltpu.VMEM((2 * block, HEAD_DIM), jnp.bfloat16),
            pltpu.VMEM((8, HEAD_DIM, TILE), jnp.bfloat16),
            pltpu.VMEM((4, 5 * TILE, TILE), jnp.float32),
            pltpu.VMEM((2, 2 * block, HEAD_DIM), jnp.float32),
            pltpu.VMEM((stacks, block, wide), jnp.bfloat16),
            pltpu.SemaphoreType.DMA((5,)),
            pltpu.SemaphoreType.DMA((8 * stacks,)),
            pltpu.SemaphoreType.DMA((stacks, 4)),
        ],
        input_output_aliases=aliases,
        compiler_params=pltpu.CompilerParams(vmem_limit_bytes=40 * 2**20),
        cost_estimate=pl.CostEstimate(
            flops=heads * 10 * 5 * 2 * 128**3,
            bytes_accessed=heads * block * HEAD_DIM * 2 * 3,
            transcendentals=heads * 10 * 128**2,
        ),
    )(*args)


def from_behind(shard, axis, by):
    length = lax.axis_size(axis)
    pairs = [(i, i + by) for i in range(length) if 0 <= i + by < length]
    return lax.ppermute(shard, axis, pairs)


def around(pieces):
    return [
        lax.ppermute(piece, "hd", [(i, (i + shift) % 4) for i in range(4)])
        for shift, piece in zip(SHIFTS, pieces)
    ]


def per_device(query, key, value, dout, doc_ids, tile_plan):
    rows = query.shape[0]
    length = 4 * rows
    index = lax.axis_index("cp")
    me = lax.axis_index("hd").reshape(1)

    got_kv = around(cut(me, key, value, 256, 0, 256))
    got = [
        around(cut(me, query, dout, 2048, (group * 8 + first) * HEAD_DIM, heads * HEAD_DIM))
        for group, first, heads in PARTS
    ]
    kv_own = join(me, got_kv, key, value)
    kv_prev = from_behind(kv_own, "cp", 1)

    own_docs = lax.dynamic_slice_in_dim(doc_ids, index * length, length, 0)
    prior_docs = lax.dynamic_slice_in_dim(
        doc_ids, jnp.maximum(index - 1, 0) * length, length, 0
    )
    plan = lax.dynamic_index_in_dim(tile_plan, index, 0, keepdims=False)
    docs = jnp.concatenate([jnp.where(index > 0, prior_docs, -1), own_docs])
    start = jnp.sum((docs[None, :] < own_docs[:, None]).astype(jnp.int32), axis=1)
    start = jnp.where(plan != 0, start, jnp.maximum(start, length))
    counts = 5 + jnp.arange(4, dtype=jnp.int32) - start[::TILE] // TILE
    scal = jnp.concatenate([me, counts])
    start = start.reshape(1, length)

    query_grad, sums = None, None
    own, prior = [], []
    for at, part in enumerate(PARTS):
        ends = at + 1 == len(PARTS) or PARTS[at + 1][0] != part[0]
        query_grad, *more = attention(
            part, scal, start, kv_own, kv_prev, got[at], query, dout, query_grad, sums, ends
        )
        if ends:
            own.append(more[0])
            prior.append(from_behind(more[1], "cp", -1))
            sums = None
        else:
            sums = more[0]
    totals = [
        jnp.concatenate(
            [(own[g][i] + prior[g][i].astype(jnp.float32)) for g in range(2)], axis=1
        ).astype(jnp.bfloat16)
        for i in range(2)
    ]
    return query_grad, totals[0], totals[1]


def solution(mesh):
    return jax.shard_map(
        per_device,
        mesh=mesh,
        in_specs=(
            P(("cp", "hd"), None),
            P(("cp", "hd"), None),
            P(("cp", "hd"), None),
            P(("cp", "hd"), None),
            P(),
            P(),
        ),
        out_specs=(P("cp", "hd"), P("cp", "hd"), P("cp", "hd")),
        check_vma=False,
    )
```

```python
import functools
import math

import jax
import jax.numpy as jnp
from jax import lax
from jax.experimental import pallas as pl
from jax.experimental.pallas import tpu as pltpu
from jax.sharding import PartitionSpec as P

HEAD_DIM = 128
TILE = 128
STACK = 4
SHIFTS = (1, -1, 2)
SENT = ((0, 8), (8, 4), (12, 4))
PARTS = ((0, 0, 8, 0), (1, 0, 4, 1), (1, 4, 4, 2))

ANY = pl.BlockSpec(memory_space=pl.ANY)
HBM = pl.BlockSpec(memory_space=pltpu.HBM)
VMEM = pl.BlockSpec(memory_space=pltpu.VMEM)
SMEM = pl.BlockSpec(memory_space=pltpu.SMEM)
ROWS_BY_ROWS = (((1,), (1,)), ((), ()))
ROWS_BY_COLUMNS = (((1,), (0,)), ((), ()))


def dot(left, right, dims):
    return lax.dot_general(left, right, dims, preferred_element_type=jnp.float32)


def aligned(index, unit):
    return pl.multiple_of(index * unit, unit)


def source_of(me, shift):
    return lax.rem(me - shift + 4, 4)


def cut_kernel(share, first, width, shifts, me_ref, left, right, *refs):
    for shift, out in zip(shifts, refs[-len(shifts) :]):
        to = lax.rem(me_ref[0] + shift + 4, 4)
        columns = pl.ds(pl.multiple_of(to * share + first, TILE), width)
        out[0] = left[:, columns]
        out[1] = right[:, columns]


def cut(name, me, left, right, share, first, width, shifts, after=()):
    rows, count = left.shape[0], len(shifts)
    shape = jax.ShapeDtypeStruct((2, rows, width), left.dtype)
    return pl.pallas_call(
        functools.partial(cut_kernel, share, first, width, shifts),
        out_shape=(shape,) * count,
        in_specs=[SMEM, VMEM, VMEM] + [ANY] * len(after),
        out_specs=(VMEM,) * count,
        cost_estimate=pl.CostEstimate(
            flops=0, bytes_accessed=4 * count * rows * width * 2, transcendentals=0
        ),
        compiler_params=pltpu.CompilerParams(vmem_limit_bytes=16 * 2**20),
        name=name,
    )(me, left, right, *after)


def open_kernel(me_ref, key, value, query, dout, *refs):
    *outs, sems = refs
    me = me_ref[0]
    copies = []
    for out, shift, pair in zip(
        outs,
        (*SHIFTS, *SHIFTS[:2], 0),
        ((key, value),) * 3 + ((query, dout),) * 3,
    ):
        to = lax.rem(me + shift + 4, 4)
        for i, array in enumerate(pair):
            columns = pl.ds(aligned(to, array.shape[1] // 4), out.shape[2])
            copies.append(
                pltpu.make_async_copy(array.at[:, columns], out.at[i], sems.at[len(copies)])
            )
    for copy in copies:
        copy.start()
    for copy in copies:
        copy.wait()


def open_cut(me, key, value, query, dout):
    rows = key.shape[0]
    shapes = [jax.ShapeDtypeStruct((2, rows, 256), key.dtype)] * 3
    shapes += [jax.ShapeDtypeStruct((2, rows, SENT[0][1] * HEAD_DIM), key.dtype)] * 3
    return pl.pallas_call(
        open_kernel,
        out_shape=tuple(shapes),
        in_specs=[SMEM] + [ANY] * 4,
        out_specs=(VMEM,) * 6,
        scratch_shapes=[pltpu.SemaphoreType.DMA((12,))],
        cost_estimate=pl.CostEstimate(flops=0, bytes_accessed=4 * 2**20, transcendentals=0),
        name="open_cut",
    )(me, key, value, query, dout)


def join_kernel(width, me_ref, got_a, got_b, got_c, left, right, out):
    me = me_ref[0]
    rows = left.shape[0]
    columns = pl.ds(aligned(me, width), width)
    for i, array in enumerate((left, right)):
        out[i, pl.ds(aligned(me, rows), rows), :] = array[:, columns]
    for shift, got in zip(SHIFTS, (got_a, got_b, got_c)):
        out[:, pl.ds(aligned(source_of(me, shift), rows), rows), :] = got[...]


def join(me, got, left, right):
    rows, width = got[0].shape[1:]
    return pl.pallas_call(
        functools.partial(join_kernel, width),
        out_shape=jax.ShapeDtypeStruct((2, 4 * rows, width), left.dtype),
        in_specs=[SMEM] + [VMEM] * 5,
        out_specs=VMEM,
        cost_estimate=pl.CostEstimate(
            flops=0, bytes_accessed=16 * rows * width * 2, transcendentals=0
        ),
        compiler_params=pltpu.CompilerParams(vmem_limit_bytes=16 * 2**20),
        name="join",
    )(me, *got, left, right)


def prepare_kernel(start, kv_own, kv_prev, kv, keys_t, bias):
    block = kv_own.shape[1]
    kv[:, :block, :] = kv_prev[...]
    kv[:, block:, :] = kv_own[...]
    for row in range(4):
        place = lax.broadcasted_iota(jnp.int32, (5 * TILE, TILE), 0) + row * TILE
        token = lax.broadcasted_iota(jnp.int32, (5 * TILE, TILE), 1) + block + row * TILE
        since = start[:, row * TILE : (row + 1) * TILE]
        bias[row] = jnp.where((place >= since) & (place <= token), 0.0, -1e30)
    for j, source in enumerate((kv_prev, kv_own)):
        for group in range(2):
            for i in range(4):
                piece = source[
                    0, i * TILE : (i + 1) * TILE, group * HEAD_DIM : (group + 1) * HEAD_DIM
                ]
                keys_t[group, 4 * j + i] = piece.T


def prepare(start, kv_own, kv_prev):
    block, width = kv_own.shape[1:]
    return pl.pallas_call(
        prepare_kernel,
        out_shape=(
            jax.ShapeDtypeStruct((2, 2 * block, width), jnp.bfloat16),
            jax.ShapeDtypeStruct((2, 8, HEAD_DIM, TILE), jnp.bfloat16),
            jax.ShapeDtypeStruct((4, 5 * TILE, TILE), jnp.float32),
        ),
        in_specs=[VMEM] * 3,
        out_specs=(VMEM,) * 3,
        cost_estimate=pl.CostEstimate(
            flops=0, bytes_accessed=8 * block * width * 2, transcendentals=0
        ),
        compiler_params=pltpu.CompilerParams(vmem_limit_bytes=16 * 2**20),
        name="prepare",
    )(start, kv_own, kv_prev)


def attention_kernel(part, begins, ends, passes, *refs):
    group, first, heads, sent = part
    offset = group * 8 + first - SENT[sent][0]
    stacks = heads // STACK
    wide = STACK * HEAD_DIM
    refs = list(refs)
    scal, *pieces, kv, keys_t, bias = refs[:8]
    refs = refs[8 + (first + group > 0) :]
    sums_in = None if begins else refs.pop(0)
    refs = refs[passes:]
    query_out, sums = refs.pop(0), refs.pop(0)
    prior_out = refs.pop(0) if ends else None
    refs = refs[passes:]
    q_all, d_all, dq, out_sems = refs
    me = scal[0]
    block = kv.shape[1] // 2
    lanes = slice(group * HEAD_DIM, (group + 1) * HEAD_DIM)

    for shift, piece in zip((*SHIFTS, 0), pieces):
        row = source_of(me, shift)
        for stack in range(stacks):
            for h in range(STACK):
                head = offset + stack * STACK + h
                columns = slice(head * HEAD_DIM, (head + 1) * HEAD_DIM)
                at = slice(h * TILE, (h + 1) * TILE)
                q_all[stack, row, at, :] = piece[0, :, columns]
                d_all[stack, row, at, :] = piece[1, :, columns]
    if begins:
        sums[...] = jnp.zeros_like(sums)
    else:
        sums[...] = sums_in[...]

    to_exponent = math.log2(math.e) / math.sqrt(HEAD_DIM)
    scale = 1.0 / math.sqrt(HEAD_DIM)

    def step(stack, row, tiles):
        tile = row + 5 - tiles
        window = pl.ds(aligned(tile, TILE), tiles * TILE)
        key, value = kv[0, window, lanes], kv[1, window, lanes]
        q, d = q_all[stack, row], d_all[stack, row]
        mask = bias[row, (5 - tiles) * TILE :, :]
        scores = dot(key, q, ROWS_BY_ROWS) * to_exponent + jnp.concatenate([mask] * STACK, axis=1)
        highest = jnp.max(scores, axis=0, keepdims=True)
        weights = jnp.exp2(scores - highest)
        probs = weights * (1.0 / jnp.sum(weights, axis=0, keepdims=True))
        dprobs = dot(value, d, ROWS_BY_ROWS)
        delta = jnp.sum(probs * dprobs, axis=0, keepdims=True)
        dscores = (probs * (dprobs - delta)).astype(jnp.bfloat16)
        sums[1, window, :] += dot(probs.astype(jnp.bfloat16), d, ROWS_BY_COLUMNS)
        sums[0, window, :] += dot(dscores, q, ROWS_BY_COLUMNS)
        key_t = jnp.concatenate([keys_t[group, tile + i] for i in range(tiles)], axis=1)
        dq_t = dot(key_t, dscores, ROWS_BY_COLUMNS) * scale
        own = pl.ds(aligned(row, TILE), TILE)
        for h in range(STACK):
            columns = slice(h * HEAD_DIM, (h + 1) * HEAD_DIM)
            dq[stack, own, columns] = dq_t[:, columns].T.astype(jnp.bfloat16)

    def out_copy(stack, row):
        own = pl.ds(aligned(row, TILE), TILE)
        column = (group * 8 + first + stack * STACK) * HEAD_DIM
        return pltpu.make_async_copy(
            dq.at[stack, own, :],
            query_out.at[own, pl.ds(column, wide)],
            out_sems.at[stack, row],
        )

    for stack in range(stacks):

        @pl.loop(0, 4)
        def _(row):
            count = scal[1 + row]
            for tiles in range(1, 6):

                @pl.when(count == tiles)
                def _():
                    step(stack, row, tiles)

            out_copy(stack, row).start()

    if ends:
        prior_out[0] = (sums[0, :block, :] * scale).astype(jnp.bfloat16)
        prior_out[1] = sums[1, :block, :].astype(jnp.bfloat16)
    for stack in range(stacks):
        for row in range(4):
            out_copy(stack, row).wait()


def attention(name, part, scal, pieces, ready, query_grad, sums, ends, passed):
    group, first, heads, sent = part
    rows = pieces[0].shape[1]
    block = 4 * rows
    stacks = heads // STACK
    wide = STACK * HEAD_DIM
    args = [scal, *pieces, *ready]
    specs = [SMEM] + [VMEM] * 7
    shapes = [jax.ShapeDtypeStruct((block, 2048), jnp.bfloat16)]
    aliases = {}
    if query_grad is not None:
        aliases[len(args)] = 0
        args.append(query_grad)
        specs.append(ANY)
    if sums is not None:
        args.append(sums)
        specs.append(VMEM)
    shapes.append(jax.ShapeDtypeStruct((2, 2 * block, HEAD_DIM), jnp.float32))
    if ends:
        shapes.append(jax.ShapeDtypeStruct((2, block, HEAD_DIM), jnp.bfloat16))
    out_specs = [ANY] + [VMEM] * (len(shapes) - 1)
    for array in passed:
        aliases[len(args)] = len(shapes)
        args.append(array)
        specs.append(ANY)
        shapes.append(jax.ShapeDtypeStruct(array.shape, array.dtype))
        out_specs.append(ANY)
    return pl.pallas_call(
        functools.partial(attention_kernel, part, sums is None, ends, len(passed)),
        out_shape=tuple(shapes),
        in_specs=specs,
        out_specs=tuple(out_specs),
        scratch_shapes=[
            pltpu.VMEM((stacks, 4, STACK * TILE, HEAD_DIM), jnp.bfloat16),
            pltpu.VMEM((stacks, 4, STACK * TILE, HEAD_DIM), jnp.bfloat16),
            pltpu.VMEM((stacks, block, wide), jnp.bfloat16),
            pltpu.SemaphoreType.DMA((stacks, 4)),
        ],
        input_output_aliases=aliases,
        compiler_params=pltpu.CompilerParams(vmem_limit_bytes=24 * 2**20),
        cost_estimate=pl.CostEstimate(
            flops=heads * 10 * 5 * 2 * 128**3,
            bytes_accessed=heads * block * HEAD_DIM * 2 * 3,
            transcendentals=heads * 10 * 128**2,
        ),
        name=name,
    )(*args)


def from_behind(shard, axis, by):
    length = lax.axis_size(axis)
    pairs = [(i, i + by) for i in range(length) if 0 <= i + by < length]
    return lax.ppermute(shard, axis, pairs)


def around(pieces):
    return [
        lax.ppermute(piece, "hd", [(i, (i + shift) % 4) for i in range(4)])
        for shift, piece in zip(SHIFTS, pieces)
    ]


def per_device(query, key, value, dout, doc_ids, tile_plan):
    rows = query.shape[0]
    length = 4 * rows
    index = lax.axis_index("cp")
    me = lax.axis_index("hd").reshape(1)

    opened = open_cut(me, key, value, query, dout)
    got_kv = around(opened[:3])
    kv_own = join(me, got_kv, key, value)
    kv_prev = from_behind(kv_own, "cp", 1)
    own_docs = lax.dynamic_slice_in_dim(doc_ids, index * length, length, 0)
    prior_docs = lax.dynamic_slice_in_dim(
        doc_ids, jnp.maximum(index - 1, 0) * length, length, 0
    )
    plan = lax.dynamic_index_in_dim(tile_plan, index, 0, keepdims=False)
    docs = jnp.concatenate([jnp.where(index > 0, prior_docs, -1), own_docs])
    start = jnp.sum((docs[None, :] < own_docs[:, None]).astype(jnp.int32), axis=1)
    start = jnp.where(plan != 0, start, jnp.maximum(start, length))
    counts = 5 + jnp.arange(4, dtype=jnp.int32) - start[::TILE] // TILE
    scal = jnp.concatenate([me, counts])
    start = start.reshape(1, length)

    ready = prepare(start, kv_own, kv_prev)

    def cut_heads(at, shifts, after):
        first, heads = SENT[at]
        name = "cut_%d" % at
        begin, width = first * HEAD_DIM, heads * HEAD_DIM
        return cut(name, me, query, dout, 2048, begin, width, shifts, after)

    *sent, own_a = opened[3:]
    sent_a = [*sent, *cut_heads(0, (2,), got_kv[:1])]
    sent, own_b = cut_heads(1, (1, 0), (kv_own,))
    sent_b = [sent, *cut_heads(1, (-1, 2), ready)]
    got_a = around(sent_a)
    *sent_c, own_c = cut_heads(2, (1, -1, 0), got_a[2:])
    pieces = [[*got_a, own_a], [*around(sent_b), own_b]]

    query_grad, sums, passed = None, None, []
    total, prior = [], []
    for at, part in enumerate(PARTS):
        ends = at + 1 == len(PARTS) or PARTS[at + 1][0] != part[0]
        query_grad, sums, *more = attention(
            "attend_%d" % at,
            part,
            scal,
            pieces[part[3]],
            ready,
            query_grad,
            sums,
            ends,
            passed,
        )
        if at == 0:
            sent_c += cut_heads(2, (2,), more)
            pieces.append([*around(sent_c), own_c])
        if passed:
            prior.append(from_behind(more.pop(), "cp", -1))
        passed = []
        if ends:
            total.append(sums[:, length:, :])
            passed = more
            sums = None
    prior.append(from_behind(passed[0], "cp", -1))
    scale = 1.0 / math.sqrt(HEAD_DIM)
    key_grad, value_grad = [
        jnp.concatenate(
            [total[g][i] * factor + prior[g][i].astype(jnp.float32) for g in range(2)], axis=1
        ).astype(jnp.bfloat16)
        for i, factor in enumerate((scale, 1.0))
    ]
    return query_grad, key_grad, value_grad


def solution(mesh):
    return jax.shard_map(
        per_device,
        mesh=mesh,
        in_specs=(
            P(("cp", "hd"), None),
            P(("cp", "hd"), None),
            P(("cp", "hd"), None),
            P(("cp", "hd"), None),
            P(),
            P(),
        ),
        out_specs=(P("cp", "hd"), P("cp", "hd"), P("cp", "hd")),
        check_vma=False,
    )
```

```python
import functools
import math

import jax
import jax.numpy as jnp
from jax import lax
from jax.experimental import pallas as pl
from jax.experimental.pallas import tpu as pltpu
from jax.sharding import PartitionSpec as P

HEAD_DIM = 128
TILE = 128
SHIFTS = (1, -1, 2)
SENT = ((0, 8), (8, 4), (12, 4))
PARTS = ((0, 0, 8, 0), (1, 0, 4, 1), (1, 4, 4, 2))

ANY = pl.BlockSpec(memory_space=pl.ANY)
HBM = pl.BlockSpec(memory_space=pltpu.HBM)
VMEM = pl.BlockSpec(memory_space=pltpu.VMEM)
SMEM = pl.BlockSpec(memory_space=pltpu.SMEM)
ROWS_BY_ROWS = (((1,), (1,)), ((), ()))
ROWS_BY_COLUMNS = (((1,), (0,)), ((), ()))


def dot(left, right, dims):
    return lax.dot_general(left, right, dims, preferred_element_type=jnp.float32)


def aligned(index, unit):
    return pl.multiple_of(index * unit, unit)


def source_of(me, shift):
    return lax.rem(me - shift + 4, 4)


def cut_kernel(share, first, width, shifts, me_ref, left, right, *refs):
    for shift, out in zip(shifts, refs[-len(shifts) :]):
        to = lax.rem(me_ref[0] + shift + 4, 4)
        columns = pl.ds(pl.multiple_of(to * share + first, TILE), width)
        out[0] = left[:, columns]
        out[1] = right[:, columns]


def cut(name, me, left, right, share, first, width, shifts, after=()):
    rows, count = left.shape[0], len(shifts)
    shape = jax.ShapeDtypeStruct((2, rows, width), left.dtype)
    return pl.pallas_call(
        functools.partial(cut_kernel, share, first, width, shifts),
        out_shape=(shape,) * count,
        in_specs=[SMEM, VMEM, VMEM] + [ANY] * len(after),
        out_specs=(VMEM,) * count,
        cost_estimate=pl.CostEstimate(
            flops=0, bytes_accessed=4 * count * rows * width * 2, transcendentals=0
        ),
        compiler_params=pltpu.CompilerParams(vmem_limit_bytes=16 * 2**20),
        name=name,
    )(me, left, right, *after)


def open_kernel(me_ref, key, value, query, dout, *refs):
    *outs, sems = refs
    me = me_ref[0]
    copies = []
    for out, shift, pair in zip(
        outs,
        (*SHIFTS, *SHIFTS[:2], 0),
        ((key, value),) * 3 + ((query, dout),) * 3,
    ):
        to = lax.rem(me + shift + 4, 4)
        for i, array in enumerate(pair):
            columns = pl.ds(aligned(to, array.shape[1] // 4), out.shape[2])
            copies.append(
                pltpu.make_async_copy(array.at[:, columns], out.at[i], sems.at[len(copies)])
            )
    for copy in copies:
        copy.start()
    for copy in copies:
        copy.wait()


def open_cut(me, key, value, query, dout):
    rows = key.shape[0]
    shapes = [jax.ShapeDtypeStruct((2, rows, 256), key.dtype)] * 3
    shapes += [jax.ShapeDtypeStruct((2, rows, SENT[0][1] * HEAD_DIM), key.dtype)] * 3
    return pl.pallas_call(
        open_kernel,
        out_shape=tuple(shapes),
        in_specs=[SMEM] + [ANY] * 4,
        out_specs=(VMEM,) * 6,
        scratch_shapes=[pltpu.SemaphoreType.DMA((12,))],
        cost_estimate=pl.CostEstimate(flops=0, bytes_accessed=4 * 2**20, transcendentals=0),
        name="open_cut",
    )(me, key, value, query, dout)


def join_kernel(width, me_ref, got_a, got_b, got_c, left, right, out):
    me = me_ref[0]
    rows = left.shape[0]
    columns = pl.ds(aligned(me, width), width)
    for i, array in enumerate((left, right)):
        out[i, pl.ds(aligned(me, rows), rows), :] = array[:, columns]
    for shift, got in zip(SHIFTS, (got_a, got_b, got_c)):
        out[:, pl.ds(aligned(source_of(me, shift), rows), rows), :] = got[...]


def join(me, got, left, right):
    rows, width = got[0].shape[1:]
    return pl.pallas_call(
        functools.partial(join_kernel, width),
        out_shape=jax.ShapeDtypeStruct((2, 4 * rows, width), left.dtype),
        in_specs=[SMEM] + [VMEM] * 5,
        out_specs=VMEM,
        cost_estimate=pl.CostEstimate(
            flops=0, bytes_accessed=16 * rows * width * 2, transcendentals=0
        ),
        compiler_params=pltpu.CompilerParams(vmem_limit_bytes=16 * 2**20),
        name="join",
    )(me, *got, left, right)


def prepare_kernel(start, kv_own, kv_prev, kv, keys_t, bias):
    block = kv_own.shape[1]
    kv[:, :block, :] = kv_prev[...]
    kv[:, block:, :] = kv_own[...]
    for row in range(4):
        place = lax.broadcasted_iota(jnp.int32, (5 * TILE, TILE), 0) + row * TILE
        token = lax.broadcasted_iota(jnp.int32, (5 * TILE, TILE), 1) + block + row * TILE
        since = start[:, row * TILE : (row + 1) * TILE]
        bias[row] = jnp.where((place >= since) & (place <= token), 0.0, -1e30)
    for j, source in enumerate((kv_prev, kv_own)):
        for group in range(2):
            for i in range(4):
                piece = source[
                    0, i * TILE : (i + 1) * TILE, group * HEAD_DIM : (group + 1) * HEAD_DIM
                ]
                keys_t[group, 4 * j + i] = piece.T


def prepare(start, kv_own, kv_prev):
    block, width = kv_own.shape[1:]
    return pl.pallas_call(
        prepare_kernel,
        out_shape=(
            jax.ShapeDtypeStruct((2, 2 * block, width), jnp.bfloat16),
            jax.ShapeDtypeStruct((2, 8, HEAD_DIM, TILE), jnp.bfloat16),
            jax.ShapeDtypeStruct((4, 5 * TILE, TILE), jnp.float32),
        ),
        in_specs=[VMEM] * 3,
        out_specs=(VMEM,) * 3,
        cost_estimate=pl.CostEstimate(
            flops=0, bytes_accessed=8 * block * width * 2, transcendentals=0
        ),
        compiler_params=pltpu.CompilerParams(vmem_limit_bytes=16 * 2**20),
        name="prepare",
    )(start, kv_own, kv_prev)


def attention_kernel(part, begins, ends, passes, *refs):
    group, first, heads, sent = part
    offset = group * 8 + first - SENT[sent][0]
    stacks = 1
    wide = heads * HEAD_DIM
    refs = list(refs)
    scal, *pieces, kv, keys_t, bias = refs[:8]
    refs = refs[8 + (first + group > 0) :]
    sums_in = None if begins else refs.pop(0)
    refs = refs[passes:]
    query_out, sums = refs.pop(0), refs.pop(0)
    prior_out = refs.pop(0) if ends else None
    refs = refs[passes:]
    q_all, d_all, dq, out_sems = refs
    me = scal[0]
    block = kv.shape[1] // 2
    lanes = slice(group * HEAD_DIM, (group + 1) * HEAD_DIM)

    for shift, piece in zip((*SHIFTS, 0), pieces):
        row = source_of(me, shift)
        for stack in range(stacks):
            for h in range(heads):
                head = offset + stack * heads + h
                columns = slice(head * HEAD_DIM, (head + 1) * HEAD_DIM)
                at = slice(h * TILE, (h + 1) * TILE)
                q_all[stack, row, at, :] = piece[0, :, columns]
                d_all[stack, row, at, :] = piece[1, :, columns]
    if begins:
        sums[...] = jnp.zeros_like(sums)
    else:
        sums[...] = sums_in[...]

    to_exponent = math.log2(math.e) / math.sqrt(HEAD_DIM)
    scale = 1.0 / math.sqrt(HEAD_DIM)

    def step(stack, row, tiles):
        tile = row + 5 - tiles
        window = pl.ds(aligned(tile, TILE), tiles * TILE)
        key, value = kv[0, window, lanes], kv[1, window, lanes]
        q, d = q_all[stack, row], d_all[stack, row]
        mask = bias[row, (5 - tiles) * TILE :, :]
        scores = dot(key, q, ROWS_BY_ROWS) * to_exponent + jnp.concatenate([mask] * heads, axis=1)
        highest = jnp.max(scores, axis=0, keepdims=True)
        weights = jnp.exp2(scores - highest)
        probs = weights * (1.0 / jnp.sum(weights, axis=0, keepdims=True))
        dprobs = dot(value, d, ROWS_BY_ROWS)
        delta = jnp.sum(probs * dprobs, axis=0, keepdims=True)
        dscores = (probs * (dprobs - delta)).astype(jnp.bfloat16)
        sums[1, window, :] += dot(probs.astype(jnp.bfloat16), d, ROWS_BY_COLUMNS)
        sums[0, window, :] += dot(dscores, q, ROWS_BY_COLUMNS)
        key_t = jnp.concatenate([keys_t[group, tile + i] for i in range(tiles)], axis=1)
        dq_t = dot(key_t, dscores, ROWS_BY_COLUMNS) * scale
        own = pl.ds(aligned(row, TILE), TILE)
        for h in range(heads):
            columns = slice(h * HEAD_DIM, (h + 1) * HEAD_DIM)
            dq[stack, own, columns] = dq_t[:, columns].T.astype(jnp.bfloat16)

    def out_copy(stack, row):
        own = pl.ds(aligned(row, TILE), TILE)
        column = (group * 8 + first + stack * heads) * HEAD_DIM
        return pltpu.make_async_copy(
            dq.at[stack, own, :],
            query_out.at[own, pl.ds(column, wide)],
            out_sems.at[stack, row],
        )

    for stack in range(stacks):

        @pl.loop(0, 4)
        def _(row):
            count = scal[1 + row]
            for tiles in range(1, 6):

                @pl.when(count == tiles)
                def _():
                    step(stack, row, tiles)

            out_copy(stack, row).start()

    if ends:
        prior_out[0] = (sums[0, :block, :] * scale).astype(jnp.bfloat16)
        prior_out[1] = sums[1, :block, :].astype(jnp.bfloat16)
    for stack in range(stacks):
        for row in range(4):
            out_copy(stack, row).wait()


def attention(name, part, scal, pieces, ready, query_grad, sums, ends, passed):
    group, first, heads, sent = part
    rows = pieces[0].shape[1]
    block = 4 * rows
    stacks = 1
    wide = heads * HEAD_DIM
    args = [scal, *pieces, *ready]
    specs = [SMEM] + [VMEM] * 7
    shapes = [jax.ShapeDtypeStruct((block, 2048), jnp.bfloat16)]
    aliases = {}
    if query_grad is not None:
        aliases[len(args)] = 0
        args.append(query_grad)
        specs.append(ANY)
    if sums is not None:
        args.append(sums)
        specs.append(VMEM)
    shapes.append(jax.ShapeDtypeStruct((2, 2 * block, HEAD_DIM), jnp.float32))
    if ends:
        shapes.append(jax.ShapeDtypeStruct((2, block, HEAD_DIM), jnp.bfloat16))
    out_specs = [ANY] + [VMEM] * (len(shapes) - 1)
    for array in passed:
        aliases[len(args)] = len(shapes)
        args.append(array)
        specs.append(ANY)
        shapes.append(jax.ShapeDtypeStruct(array.shape, array.dtype))
        out_specs.append(ANY)
    return pl.pallas_call(
        functools.partial(attention_kernel, part, sums is None, ends, len(passed)),
        out_shape=tuple(shapes),
        in_specs=specs,
        out_specs=tuple(out_specs),
        scratch_shapes=[
            pltpu.VMEM((stacks, 4, heads * TILE, HEAD_DIM), jnp.bfloat16),
            pltpu.VMEM((stacks, 4, heads * TILE, HEAD_DIM), jnp.bfloat16),
            pltpu.VMEM((stacks, block, wide), jnp.bfloat16),
            pltpu.SemaphoreType.DMA((stacks, 4)),
        ],
        input_output_aliases=aliases,
        compiler_params=pltpu.CompilerParams(vmem_limit_bytes=24 * 2**20),
        cost_estimate=pl.CostEstimate(
            flops=heads * 10 * 5 * 2 * 128**3,
            bytes_accessed=heads * block * HEAD_DIM * 2 * 3,
            transcendentals=heads * 10 * 128**2,
        ),
        name=name,
    )(*args)


def from_behind(shard, axis, by):
    length = lax.axis_size(axis)
    pairs = [(i, i + by) for i in range(length) if 0 <= i + by < length]
    return lax.ppermute(shard, axis, pairs)


def around(pieces):
    return [
        lax.ppermute(piece, "hd", [(i, (i + shift) % 4) for i in range(4)])
        for shift, piece in zip(SHIFTS, pieces)
    ]


def per_device(query, key, value, dout, doc_ids, tile_plan):
    rows = query.shape[0]
    length = 4 * rows
    index = lax.axis_index("cp")
    me = lax.axis_index("hd").reshape(1)

    opened = open_cut(me, key, value, query, dout)
    got_kv = around(opened[:3])
    kv_own = join(me, got_kv, key, value)
    kv_prev = from_behind(kv_own, "cp", 1)
    own_docs = lax.dynamic_slice_in_dim(doc_ids, index * length, length, 0)
    prior_docs = lax.dynamic_slice_in_dim(
        doc_ids, jnp.maximum(index - 1, 0) * length, length, 0
    )
    plan = lax.dynamic_index_in_dim(tile_plan, index, 0, keepdims=False)
    docs = jnp.concatenate([jnp.where(index > 0, prior_docs, -1), own_docs])
    start = jnp.sum((docs[None, :] < own_docs[:, None]).astype(jnp.int32), axis=1)
    start = jnp.where(plan != 0, start, jnp.maximum(start, length))
    counts = 5 + jnp.arange(4, dtype=jnp.int32) - start[::TILE] // TILE
    scal = jnp.concatenate([me, counts])
    start = start.reshape(1, length)

    ready = prepare(start, kv_own, kv_prev)

    def cut_heads(at, shifts, after):
        first, heads = SENT[at]
        name = "cut_%d" % at
        begin, width = first * HEAD_DIM, heads * HEAD_DIM
        return cut(name, me, query, dout, 2048, begin, width, shifts, after)

    *sent, own_a = opened[3:]
    sent_a = [*sent, *cut_heads(0, (2,), got_kv[:1])]
    *sent_b, own_b = cut_heads(1, (1, -1, 2, 0), ready)
    got_a = around(sent_a)
    *sent_c, own_c = cut_heads(2, (1, -1, 0), got_a[:1])
    pieces = [[*got_a, own_a], [*around(sent_b), own_b]]

    query_grad, sums, passed = None, None, []
    total, prior = [], []
    for at, part in enumerate(PARTS):
        ends = at + 1 == len(PARTS) or PARTS[at + 1][0] != part[0]
        query_grad, sums, *more = attention(
            "attend_%d" % at,
            part,
            scal,
            pieces[part[3]],
            ready,
            query_grad,
            sums,
            ends,
            passed,
        )
        if at == 0:
            sent_c += cut_heads(2, (2,), more)
            pieces.append([*around(sent_c), own_c])
        if passed:
            prior.append(from_behind(more.pop(), "cp", -1))
        passed = []
        if ends:
            total.append(sums[:, length:, :])
            passed = more
            sums = None
    prior.append(from_behind(passed[0], "cp", -1))
    scale = 1.0 / math.sqrt(HEAD_DIM)
    key_grad, value_grad = [
        jnp.concatenate(
            [total[g][i] * factor + prior[g][i].astype(jnp.float32) for g in range(2)], axis=1
        ).astype(jnp.bfloat16)
        for i, factor in enumerate((scale, 1.0))
    ]
    return query_grad, key_grad, value_grad


def solution(mesh):
    return jax.shard_map(
        per_device,
        mesh=mesh,
        in_specs=(
            P(("cp", "hd"), None),
            P(("cp", "hd"), None),
            P(("cp", "hd"), None),
            P(("cp", "hd"), None),
            P(),
            P(),
        ),
        out_specs=(P("cp", "hd"), P("cp", "hd"), P("cp", "hd")),
        check_vma=False,
    )
```

```python
import functools
import math

import jax
import jax.numpy as jnp
from jax import lax
from jax.experimental import pallas as pl
from jax.experimental.pallas import tpu as pltpu
from jax.sharding import PartitionSpec as P

HEAD_DIM = 128
TILE = 128
SHIFTS = (1, -1, 2)
SENT = ((0, 8), (8, 4), (12, 4))
PARTS = ((0, 0, 8, 0), (1, 0, 4, 1), (1, 4, 4, 2))

ANY = pl.BlockSpec(memory_space=pl.ANY)
HBM = pl.BlockSpec(memory_space=pltpu.HBM)
VMEM = pl.BlockSpec(memory_space=pltpu.VMEM)
SMEM = pl.BlockSpec(memory_space=pltpu.SMEM)
ROWS_BY_ROWS = (((1,), (1,)), ((), ()))
ROWS_BY_COLUMNS = (((1,), (0,)), ((), ()))


def dot(left, right, dims):
    return lax.dot_general(left, right, dims, preferred_element_type=jnp.float32)


def aligned(index, unit):
    return pl.multiple_of(index * unit, unit)


def source_of(me, shift):
    return lax.rem(me - shift + 4, 4)


def cut_kernel(share, first, width, shifts, me_ref, left, right, *refs):
    for shift, out in zip(shifts, refs[-len(shifts) :]):
        to = lax.rem(me_ref[0] + shift + 4, 4)
        columns = pl.ds(pl.multiple_of(to * share + first, TILE), width)
        out[0] = left[:, columns]
        out[1] = right[:, columns]


def cut(name, me, left, right, share, first, width, shifts, after=()):
    rows, count = left.shape[0], len(shifts)
    shape = jax.ShapeDtypeStruct((2, rows, width), left.dtype)
    return pl.pallas_call(
        functools.partial(cut_kernel, share, first, width, shifts),
        out_shape=(shape,) * count,
        in_specs=[SMEM, VMEM, VMEM] + [ANY] * len(after),
        out_specs=(VMEM,) * count,
        cost_estimate=pl.CostEstimate(
            flops=0, bytes_accessed=4 * count * rows * width * 2, transcendentals=0
        ),
        compiler_params=pltpu.CompilerParams(vmem_limit_bytes=16 * 2**20),
        name=name,
    )(me, left, right, *after)


def open_kernel(me_ref, key, value, query, dout, *refs):
    *outs, sems = refs
    me = me_ref[0]
    copies = []
    for out, shift, pair in zip(
        outs,
        (*SHIFTS, *SHIFTS[:2], 0),
        ((key, value),) * 3 + ((query, dout),) * 3,
    ):
        to = lax.rem(me + shift + 4, 4)
        for i, array in enumerate(pair):
            columns = pl.ds(aligned(to, array.shape[1] // 4), out.shape[2])
            copies.append(
                pltpu.make_async_copy(array.at[:, columns], out.at[i], sems.at[len(copies)])
            )
    for copy in copies:
        copy.start()
    for copy in copies:
        copy.wait()


def open_cut(me, key, value, query, dout):
    rows = key.shape[0]
    shapes = [jax.ShapeDtypeStruct((2, rows, 256), key.dtype)] * 3
    shapes += [jax.ShapeDtypeStruct((2, rows, SENT[0][1] * HEAD_DIM), key.dtype)] * 3
    return pl.pallas_call(
        open_kernel,
        out_shape=tuple(shapes),
        in_specs=[SMEM] + [ANY] * 4,
        out_specs=(VMEM,) * 6,
        scratch_shapes=[pltpu.SemaphoreType.DMA((12,))],
        cost_estimate=pl.CostEstimate(flops=0, bytes_accessed=4 * 2**20, transcendentals=0),
        name="open_cut",
    )(me, key, value, query, dout)


def join_kernel(width, me_ref, got_a, got_b, got_c, left, right, out):
    me = me_ref[0]
    rows = left.shape[0]
    columns = pl.ds(aligned(me, width), width)
    for i, array in enumerate((left, right)):
        out[i, pl.ds(aligned(me, rows), rows), :] = array[:, columns]
    for shift, got in zip(SHIFTS, (got_a, got_b, got_c)):
        out[:, pl.ds(aligned(source_of(me, shift), rows), rows), :] = got[...]


def join(me, got, left, right):
    rows, width = got[0].shape[1:]
    return pl.pallas_call(
        functools.partial(join_kernel, width),
        out_shape=jax.ShapeDtypeStruct((2, 4 * rows, width), left.dtype),
        in_specs=[SMEM] + [VMEM] * 5,
        out_specs=VMEM,
        cost_estimate=pl.CostEstimate(
            flops=0, bytes_accessed=16 * rows * width * 2, transcendentals=0
        ),
        compiler_params=pltpu.CompilerParams(vmem_limit_bytes=16 * 2**20),
        name="join",
    )(me, *got, left, right)


def prepare_kernel(start, kv_own, kv_prev, kv, keys_t, bias):
    block = kv_own.shape[1]
    kv[:, :block, :] = kv_prev[...]
    kv[:, block:, :] = kv_own[...]
    for row in range(4):
        place = lax.broadcasted_iota(jnp.int32, (5 * TILE, TILE), 0) + row * TILE
        token = lax.broadcasted_iota(jnp.int32, (5 * TILE, TILE), 1) + block + row * TILE
        since = start[:, row * TILE : (row + 1) * TILE]
        bias[row] = jnp.where((place >= since) & (place <= token), 0.0, -1e30)
    for j, source in enumerate((kv_prev, kv_own)):
        for group in range(2):
            for i in range(4):
                piece = source[
                    0, i * TILE : (i + 1) * TILE, group * HEAD_DIM : (group + 1) * HEAD_DIM
                ]
                keys_t[group, 4 * j + i] = piece.T


def prepare(start, kv_own, kv_prev):
    block, width = kv_own.shape[1:]
    return pl.pallas_call(
        prepare_kernel,
        out_shape=(
            jax.ShapeDtypeStruct((2, 2 * block, width), jnp.bfloat16),
            jax.ShapeDtypeStruct((2, 8, HEAD_DIM, TILE), jnp.bfloat16),
            jax.ShapeDtypeStruct((4, 5 * TILE, TILE), jnp.float32),
        ),
        in_specs=[VMEM] * 3,
        out_specs=(VMEM,) * 3,
        cost_estimate=pl.CostEstimate(
            flops=0, bytes_accessed=8 * block * width * 2, transcendentals=0
        ),
        compiler_params=pltpu.CompilerParams(vmem_limit_bytes=16 * 2**20),
        name="prepare",
    )(start, kv_own, kv_prev)


def attention_kernel(part, begins, ends, passes, *refs):
    group, first, heads, sent = part
    offset = group * 8 + first - SENT[sent][0]
    stacks = 1
    wide = heads * HEAD_DIM
    refs = list(refs)
    scal, *pieces, kv, keys_t, bias = refs[:8]
    refs = refs[8 + (first + group > 0) :]
    sums_in = None if begins else refs.pop(0)
    refs = refs[passes:]
    query_out, sums = refs.pop(0), refs.pop(0)
    prior_out = refs.pop(0) if ends else None
    refs = refs[passes:]
    q_all, d_all, dq, out_sems = refs
    me = scal[0]
    block = kv.shape[1] // 2
    lanes = slice(group * HEAD_DIM, (group + 1) * HEAD_DIM)

    for shift, piece in zip((*SHIFTS, 0), pieces):
        row = source_of(me, shift)
        for stack in range(stacks):
            for h in range(heads):
                head = offset + stack * heads + h
                columns = slice(head * HEAD_DIM, (head + 1) * HEAD_DIM)
                at = slice(h * TILE, (h + 1) * TILE)
                q_all[stack, row, at, :] = piece[0, :, columns]
                d_all[stack, row, at, :] = piece[1, :, columns]
    if begins:
        sums[...] = jnp.zeros_like(sums)
    else:
        sums[...] = sums_in[...]

    to_exponent = math.log2(math.e) / math.sqrt(HEAD_DIM)
    scale = 1.0 / math.sqrt(HEAD_DIM)

    def step(stack, row, tiles):
        tile = row + 5 - tiles
        window = pl.ds(aligned(tile, TILE), tiles * TILE)
        key, value = kv[0, window, lanes], kv[1, window, lanes]
        q, d = q_all[stack, row], d_all[stack, row]
        mask = bias[row, (5 - tiles) * TILE :, :]
        scores = dot(key, q, ROWS_BY_ROWS) * to_exponent + jnp.concatenate([mask] * heads, axis=1)
        highest = jnp.max(scores, axis=0, keepdims=True)
        weights = jnp.exp2(scores - highest)
        probs = weights * (1.0 / jnp.sum(weights, axis=0, keepdims=True))
        dprobs = dot(value, d, ROWS_BY_ROWS)
        delta = jnp.sum(probs * dprobs, axis=0, keepdims=True)
        dscores = (probs * (dprobs - delta)).astype(jnp.bfloat16)
        sums[1, window, :] += dot(probs.astype(jnp.bfloat16), d, ROWS_BY_COLUMNS)
        sums[0, window, :] += dot(dscores, q, ROWS_BY_COLUMNS)
        key_t = jnp.concatenate([keys_t[group, tile + i] for i in range(tiles)], axis=1)
        dq_t = dot(key_t, dscores, ROWS_BY_COLUMNS) * scale
        own = pl.ds(aligned(row, TILE), TILE)
        for h in range(heads):
            columns = slice(h * HEAD_DIM, (h + 1) * HEAD_DIM)
            dq[stack, own, columns] = dq_t[:, columns].T.astype(jnp.bfloat16)

    def out_copy(stack, row):
        own = pl.ds(aligned(row, TILE), TILE)
        column = (group * 8 + first + stack * heads) * HEAD_DIM
        return pltpu.make_async_copy(
            dq.at[stack, own, :],
            query_out.at[own, pl.ds(column, wide)],
            out_sems.at[stack, row],
        )

    for stack in range(stacks):

        @pl.loop(0, 4)
        def _(row):
            count = scal[1 + row]
            for tiles in range(1, 6):

                @pl.when(count == tiles)
                def _():
                    step(stack, row, tiles)

            out_copy(stack, row).start()

    if ends:
        prior_out[0] = (sums[0, :block, :] * scale).astype(jnp.bfloat16)
        prior_out[1] = sums[1, :block, :].astype(jnp.bfloat16)
    for stack in range(stacks):
        for row in range(4):
            out_copy(stack, row).wait()


def attention(name, part, scal, pieces, ready, query_grad, sums, ends, passed):
    group, first, heads, sent = part
    rows = pieces[0].shape[1]
    block = 4 * rows
    stacks = 1
    wide = heads * HEAD_DIM
    args = [scal, *pieces, *ready]
    specs = [SMEM] + [VMEM] * 7
    shapes = [jax.ShapeDtypeStruct((block, 2048), jnp.bfloat16)]
    aliases = {}
    if query_grad is not None:
        aliases[len(args)] = 0
        args.append(query_grad)
        specs.append(ANY)
    if sums is not None:
        args.append(sums)
        specs.append(VMEM)
    shapes.append(jax.ShapeDtypeStruct((2, 2 * block, HEAD_DIM), jnp.float32))
    if ends:
        shapes.append(jax.ShapeDtypeStruct((2, block, HEAD_DIM), jnp.bfloat16))
    out_specs = [ANY] + [VMEM] * (len(shapes) - 1)
    for array in passed:
        aliases[len(args)] = len(shapes)
        args.append(array)
        specs.append(ANY)
        shapes.append(jax.ShapeDtypeStruct(array.shape, array.dtype))
        out_specs.append(ANY)
    return pl.pallas_call(
        functools.partial(attention_kernel, part, sums is None, ends, len(passed)),
        out_shape=tuple(shapes),
        in_specs=specs,
        out_specs=tuple(out_specs),
        scratch_shapes=[
            pltpu.VMEM((stacks, 4, heads * TILE, HEAD_DIM), jnp.bfloat16),
            pltpu.VMEM((stacks, 4, heads * TILE, HEAD_DIM), jnp.bfloat16),
            pltpu.VMEM((stacks, block, wide), jnp.bfloat16),
            pltpu.SemaphoreType.DMA((stacks, 4)),
        ],
        input_output_aliases=aliases,
        compiler_params=pltpu.CompilerParams(vmem_limit_bytes=24 * 2**20),
        cost_estimate=pl.CostEstimate(
            flops=heads * 10 * 5 * 2 * 128**3,
            bytes_accessed=heads * block * HEAD_DIM * 2 * 3,
            transcendentals=heads * 10 * 128**2,
        ),
        name=name,
    )(*args)


def from_behind(shard, axis, by):
    length = lax.axis_size(axis)
    pairs = [(i, i + by) for i in range(length) if 0 <= i + by < length]
    return lax.ppermute(shard, axis, pairs)


def around(pieces):
    return [
        lax.ppermute(piece, "hd", [(i, (i + shift) % 4) for i in range(4)])
        for shift, piece in zip(SHIFTS, pieces)
    ]


def per_device(query, key, value, dout, doc_ids, tile_plan):
    rows = query.shape[0]
    length = 4 * rows
    index = lax.axis_index("cp")
    me = lax.axis_index("hd").reshape(1)

    opened = open_cut(me, key, value, query, dout)
    got_kv = around(opened[:3])
    kv_own = join(me, got_kv, key, value)
    kv_prev = from_behind(kv_own, "cp", 1)
    own_docs = lax.dynamic_slice_in_dim(doc_ids, index * length, length, 0)
    prior_docs = lax.dynamic_slice_in_dim(
        doc_ids, jnp.maximum(index - 1, 0) * length, length, 0
    )
    plan = lax.dynamic_index_in_dim(tile_plan, index, 0, keepdims=False)
    docs = jnp.concatenate([jnp.where(index > 0, prior_docs, -1), own_docs])
    start = jnp.sum((docs[None, :] < own_docs[:, None]).astype(jnp.int32), axis=1)
    start = jnp.where(plan != 0, start, jnp.maximum(start, length))
    counts = 5 + jnp.arange(4, dtype=jnp.int32) - start[::TILE] // TILE
    scal = jnp.concatenate([me, counts])
    start = start.reshape(1, length)

    ready = prepare(start, kv_own, kv_prev)

    def cut_heads(at, shifts, after):
        first, heads = SENT[at]
        name = "cut_%d" % at
        begin, width = first * HEAD_DIM, heads * HEAD_DIM
        return cut(name, me, query, dout, 2048, begin, width, shifts, after)

    *sent, own_a = opened[3:]
    sent_a = [*sent, *cut_heads(0, (2,), got_kv[:1])]
    *sent_b, own_b = cut_heads(1, (1, -1, 2, 0), ready)
    got_a = around(sent_a)
    *sent_c, own_c = cut_heads(2, (1, -1, 0), got_a[:1])
    pieces = [[*got_a, own_a], [*around(sent_b), own_b]]

    query_grad, sums, kept = None, None, []
    total = []
    for at, part in enumerate(PARTS):
        ends = at + 1 == len(PARTS) or PARTS[at + 1][0] != part[0]
        query_grad, sums, *more = attention(
            "attend_%d" % at,
            part,
            scal,
            pieces[part[3]],
            ready,
            query_grad,
            sums,
            ends,
            kept if at + 1 == len(PARTS) else [],
        )
        if at == 0:
            sent_c += cut_heads(2, (2,), more)
            pieces.append([*around(sent_c), own_c])
        if ends:
            total.append(sums[:, length:, :])
            sums = None
            if at + 1 < len(PARTS):
                kept = more
            else:
                prior = [from_behind(more.pop(), "cp", -1)]
                passed = more
    prior.append(from_behind(passed[0], "cp", -1))
    scale = 1.0 / math.sqrt(HEAD_DIM)
    key_grad, value_grad = [
        jnp.concatenate(
            [total[g][i] * factor + prior[g][i].astype(jnp.float32) for g in range(2)], axis=1
        ).astype(jnp.bfloat16)
        for i, factor in enumerate((scale, 1.0))
    ]
    return query_grad, key_grad, value_grad


def solution(mesh):
    return jax.shard_map(
        per_device,
        mesh=mesh,
        in_specs=(
            P(("cp", "hd"), None),
            P(("cp", "hd"), None),
            P(("cp", "hd"), None),
            P(("cp", "hd"), None),
            P(),
            P(),
        ),
        out_specs=(P("cp", "hd"), P("cp", "hd"), P("cp", "hd")),
        check_vma=False,
    )
```
